1024 devices in a mesh: node: 64 (over z, y), local: 16 (over x, core).
Axes of the slice: x: 8, y: 8, z: 8, core: 2. Of those that a mesh axis runs over, the one named last changes fastest.
Arguments:
- tokens: bfloat16 [8192, 7168], P('node', 'local'), may hold values from -6 to 6
- route_expert: int32 [8192], P('node'), may hold values from 0 to 15, as said below
- hidden_grad: bfloat16 [8192, 2048], P('node'), may hold values from -6 to 6
- gate_weight: bfloat16 [7168, 32768], P('local', 'node'), may hold values from -0.0625 to 0.0625
- up_weight: bfloat16 [7168, 32768], P('local', 'node'), may hold values from -0.0625 to 0.0625
Outputs:
- token_grad: bfloat16 [8192, 7168], P('node', 'local')
- gate_grad: float32 [7168, 32768], P('local', 'node')
- up_grad: float32 [7168, 32768], P('local', 'node')
The draws below stay inside these ranges and needn't reach their ends.
Inputs may be any that keep to these rules, and one draw needn't show every extreme that they name: `route_expert`: at most 10 of the 128 tokens of one index of node name the same expert; on every index of node exactly 10 of its tokens name one expert, the same expert on all of them.
All inputs are finite; a program needn't handle non-finite values.
Results may differ from the reference program's by a relative error of at most 0.0058.
Values may be sent and summed in bfloat16 or wider, within the bound.
A program may use at most 32 MiB of HBM per device.

```python
import jax
import jax.numpy as jnp
from jax import lax

D = 7168
HID = 2048
GROUP = 4
TOK_NODE = 128
EXPERTS = 16
CAP = 10
TOKENS = 8192
N_NODE = 64


def draw_route_expert(key, part):
    key = jax.random.fold_in(key, 7)
    hot_expert = jax.random.randint(jax.random.fold_in(key, 1), (), 0, EXPERTS).astype(jnp.int32)
    block_count = TOKENS // TOK_NODE

    def one_block(block_key):
        first_key, second_key = jax.random.split(block_key)
        others = jax.random.permutation(first_key, max((EXPERTS - 1) * CAP, 1)).astype(jnp.int32)
        other_expert = others // CAP
        other_expert = other_expert + (other_expert >= hot_expert).astype(jnp.int32)
        chosen = jnp.concatenate([jnp.full((CAP,), 0, jnp.int32) + hot_expert, other_expert[:TOK_NODE - CAP]])
        order = jax.random.permutation(second_key, TOK_NODE)
        return chosen[order]
    block_keys = jax.random.split(jax.random.fold_in(key, 2), block_count)
    return jax.vmap(one_block)(block_keys).reshape(TOKENS).astype(jnp.int32)


def level_of(stream_key, shape, shards, least, largest):
    def one(axis_at, blocks):
        steps = jax.random.uniform(jax.random.fold_in(jax.random.fold_in(stream_key, 6), axis_at), (blocks,), jnp.float32, least / len(shards), largest / len(shards))
        return jnp.repeat(jnp.exp(steps), shape[axis_at] // blocks).reshape((-1,) + (1,) * (len(shape) - axis_at - 1))

    level = one(*shards[0])
    for cut in shards[1:]:
        level = level * one(*cut)
    return level


def noise(rng, extent, width, limit, pieces=(), held_as=jnp.bfloat16):
    factor_of = level_of(rng, extent, pieces, -0.22, 0.18) if pieces else 1.0
    values = jax.random.normal(rng, extent, jnp.float32) * width * factor_of
    return jnp.minimum(jnp.maximum(values, -limit), limit).astype(held_as)


def setup_inputs(seed: int = 0) -> dict:
    key_of = jax.random.split(jax.random.key(seed), 6)
    tokens = noise(key_of[0], (TOKENS, D), 1.0, 6.0, ((0, 64), (1, 16)))
    route_expert = draw_route_expert(jax.random.fold_in(key_of[5], 71), 0)
    hidden_grad = noise(key_of[2], (TOKENS, HID), 1.0, 6.0, ((0, 64),))
    gate_weight = noise(key_of[3], (D, EXPERTS * HID), D ** -0.5, 0.0625, ((0, 16), (1, 64)))
    up_weight = noise(key_of[4], (D, EXPERTS * HID), D ** -0.5, 0.0625, ((0, 16), (1, 64)))
    return {"tokens": tokens, "route_expert": route_expert, "hidden_grad": hidden_grad, "gate_weight": gate_weight, "up_weight": up_weight}


def reference(tokens, route_expert, hidden_grad, gate_weight, up_weight):
    part_width = HID // GROUP
    block_rows = N_NODE * CAP
    source_node = jnp.arange(TOKENS, dtype=jnp.int32) // TOK_NODE
    bucket = route_expert * N_NODE + source_node
    onehot = (bucket[:, None] == jnp.arange(EXPERTS * N_NODE, dtype=jnp.int32)[None, :]).astype(jnp.int32)
    rank_of = jnp.sum((jnp.cumsum(onehot, axis=0) - onehot) * onehot, axis=1)
    slot_of = (bucket * CAP + rank_of).astype(jnp.int32)
    total_rows = EXPERTS * block_rows
    placed_x = jnp.zeros((total_rows, D), jnp.bfloat16).at[slot_of].set(tokens)
    placed_h = jnp.zeros((total_rows, HID), jnp.bfloat16).at[slot_of].set(hidden_grad)
    contract_cols = (((1,), (1,)), ((), ()))
    contract_rows = (((0,), (0,)), ((), ()))
    row_grads = []
    gate_parts = []
    up_parts = []
    for expert in range(EXPERTS):
        rows_x = placed_x[expert * block_rows:(expert + 1) * block_rows]
        rows_h = placed_h[expert * block_rows:(expert + 1) * block_rows].astype(jnp.float32)
        w_gate = gate_weight[:, expert * HID:(expert + 1) * HID]
        w_up = up_weight[:, expert * HID:(expert + 1) * HID]
        gate_pre = jnp.dot(rows_x, w_gate, preferred_element_type=jnp.float32)
        up_pre = jnp.dot(rows_x, w_up, preferred_element_type=jnp.float32)
        sigmoid_gate = jax.nn.sigmoid(gate_pre)
        activated = gate_pre * sigmoid_gate
        slope_gate = sigmoid_gate * (1.0 + gate_pre * (1.0 - sigmoid_gate))
        grad_up = (rows_h * activated).astype(jnp.bfloat16)
        grad_gate = (rows_h * up_pre * slope_gate).astype(jnp.bfloat16)
        accum = jnp.zeros((block_rows, D), jnp.float32)
        for block in range(GROUP):
            lower = block * part_width
            upper = lower + part_width
            piece_sum = lax.dot_general(grad_gate[:, lower:upper], w_gate[:, lower:upper], contract_cols, preferred_element_type=jnp.float32)
            piece_sum = piece_sum + lax.dot_general(grad_up[:, lower:upper], w_up[:, lower:upper], contract_cols, preferred_element_type=jnp.float32)
            accum = accum + lax.optimization_barrier(piece_sum.astype(jnp.bfloat16)).astype(jnp.float32)
        row_grads.append(accum)
        joined = jnp.concatenate([grad_gate, grad_up], axis=1)
        weight_sum = lax.dot_general(rows_x, joined, contract_rows, preferred_element_type=jnp.float32)
        gate_parts.append(weight_sum[:, :HID])
        up_parts.append(weight_sum[:, HID:])
    all_rows = jnp.concatenate(row_grads, axis=0)
    token_grad = jnp.take(all_rows, slot_of, axis=0).astype(jnp.bfloat16)
    gate_grad = jnp.concatenate(gate_parts, axis=1)
    up_grad = jnp.concatenate(up_parts, axis=1)
    return token_grad, gate_grad, up_grad
```

```python
import functools

import jax
import jax.numpy as jnp
from jax import lax
from jax.experimental import pallas as pl
from jax.experimental.pallas import tpu as pltpu
from jax.sharding import PartitionSpec as P

MESH = pl.DeviceIdType.MESH
BF = jnp.bfloat16
F32 = jnp.float32

NZ, NY, NX = 8, 8, 8
GROUP = 4
HALVES = NY // GROUP
CAP = 10
SLOT = 16
FEAT = 448
ROW = 512
HALF = 64
LANE = 128
BLOCK = NZ * CAP
ZROWS = HALVES * SLOT
ZWIDE = ROW + GROUP * HALF
WIDE = NX * LANE
PAIRS = NY // 2
EXPERTS = NZ * HALVES


def iota(shape, dim):
    return lax.broadcasted_iota(jnp.int32, shape, dim)


def dot(a, b, dims=(((1,), (0,)), ((), ()))):
    return lax.dot_general(a, b, dims, preferred_element_type=F32)


def kernel(
    route_ref, tok_ref, hid_ref, gw_ref, uw_ref,
    tg_ref, gg_ref, ug_ref,
    w_ref, zsend, zrecv, ysend, yrecv, sib_out, sib_in, rsum, rsend, rrecv, gath, yout, yret, zout, zret,
    zs_s, zs_r, ys_s, ys_r, sb_s, sb_r, rs_s, rs_r, ag_s, ag_r, rl_s, rl_r, yo_s, yo_r, zo_s, zo_r,
):
    node, local = lax.axis_index("node"), lax.axis_index("local")
    z, y = node // NY, node % NY
    x, c = local // 2, local % 2

    def at_z(d):
        return (((z + d) % NZ) * NY + y, local)

    def at_y(d):
        return (z * NY + (y + d) % NY, local)

    def at_x(d):
        return (node, ((x + d) % NX) * 2 + c)

    sibling = (node, x * 2 + 1 - c)

    def remote(src, dst, s_sem, r_sem, device):
        return pltpu.make_async_remote_copy(
            src_ref=src, dst_ref=dst, send_sem=s_sem, recv_sem=r_sem, device_id=device, device_id_type=MESH
        )

    barrier = pltpu.get_barrier_semaphore()
    for d in range(1, NZ):
        pl.semaphore_signal(barrier, inc=1, device_id=at_z(d), device_id_type=MESH)
    for d in range(1, NY):
        pl.semaphore_signal(barrier, inc=1, device_id=at_y(d), device_id_type=MESH)
    for d in range(1, NX):
        pl.semaphore_signal(barrier, inc=1, device_id=at_x(d), device_id_type=MESH)
    pl.semaphore_signal(barrier, inc=1, device_id=sibling, device_id_type=MESH)

    tok_count = tok_ref.shape[0]
    route = route_ref[...]
    onehot = (iota((EXPERTS, tok_count), 0) == route).astype(F32)
    before = (iota((tok_count, tok_count), 0) < iota((tok_count, tok_count), 1)).astype(BF)
    prior = dot(onehot.astype(BF), before)
    rank = jnp.sum(prior * onehot, axis=0, keepdims=True).astype(jnp.int32)
    slot = route * SLOT + rank
    select = (iota((EXPERTS * SLOT, tok_count), 0) == slot).astype(BF)

    odd = x % 2
    hidden = []
    for g in range(GROUP):
        start = pl.multiple_of(g * (NX * HALF) + (x // 2) * LANE, LANE)
        hidden.append(hid_ref[:, pl.ds(start, LANE)])
    low = iota((LANE, LANE), 0) == iota((LANE, LANE), 1) + HALF * odd
    high = iota((LANE, LANE), 0) == iota((LANE, LANE), 1) - HALF + HALF * odd
    place_low = (low & (iota((LANE, LANE), 1) < HALF)).astype(BF)
    place_high = (high & (iota((LANE, LANE), 1) >= HALF)).astype(BF)

    feat_rows = dot(select, tok_ref[...]).astype(BF)
    hidden_rows = []
    for g in range(0, GROUP, 2):
        both = (dot(hidden[g], place_low) + dot(hidden[g + 1], place_high)).astype(BF)
        hidden_rows.append(dot(select, both).astype(BF))
    for zz in range(NZ):
        rows = slice(zz * ZROWS, (zz + 1) * ZROWS)
        zsend[zz, :, 0:FEAT] = feat_rows[rows]
        zsend[zz, :, FEAT:ROW] = jnp.zeros((ZROWS, ROW - FEAT), BF)
        for i in range(GROUP // 2):
            zsend[zz, :, ROW + i * LANE : ROW + (i + 1) * LANE] = hidden_rows[i][rows]

    pl.semaphore_wait(barrier, (NZ - 1) + (NY - 1) + (NX - 1) + 1)

    def z_copy(d):
        return remote(zsend.at[(z + d) % NZ], zrecv.at[z], zs_s.at[d], zs_r.at[d], at_z(d))

    for d in range(1, NZ):
        z_copy(d).start()
    zrecv[z] = zsend[z]

    for i in range(NX // 2):
        g_part = gw_ref[:, i * LANE : (i + 1) * LANE]
        u_part = uw_ref[:, i * LANE : (i + 1) * LANE]
        w_ref[0:FEAT, 2 * i * LANE : (2 * i + 1) * LANE] = jnp.concatenate([g_part[:, :HALF], u_part[:, :HALF]], axis=1)
        w_ref[0:FEAT, (2 * i + 1) * LANE : (2 * i + 2) * LANE] = jnp.concatenate([g_part[:, HALF:], u_part[:, HALF:]], axis=1)
    w_ref[FEAT:ROW, :] = jnp.zeros((ROW - FEAT, WIDE), BF)

    out_i = iota((HALVES * BLOCK, NZ * ZROWS), 0)
    in_i = iota((HALVES * BLOCK, NZ * ZROWS), 1)
    out_h = out_i // BLOCK
    out_z = (out_i % BLOCK) // CAP
    compact = (in_i == out_z * ZROWS + out_h * SLOT + out_i % CAP).astype(BF)

    for d in range(1, NZ):
        z_copy(d).wait_recv()
    rows_in = zrecv[...].reshape(NZ * ZROWS, ZWIDE)
    packed = dot(compact, rows_in).astype(BF)
    for h in range(HALVES):
        part = packed[h * BLOCK : (h + 1) * BLOCK]
        for g in range(GROUP):
            ysend[h * GROUP + g, :, 0 : ROW - LANE] = part[:, 0 : ROW - LANE]
            ysend[h * GROUP + g, :, ROW - LANE : ROW] = jnp.concatenate(
                [part[:, ROW - LANE : FEAT], part[:, ROW + g * HALF : ROW + (g + 1) * HALF]], axis=1
            )

    def y_copy(d):
        return remote(ysend.at[(y + d) % NY], yrecv.at[NY - d], ys_s.at[d], ys_r.at[d], at_y(d))

    for d in (7, 1, 6, 2, 5, 3, 4):
        y_copy(d).start()
    yrecv[0] = ysend[y]

    def slots(p):
        a, b = (NY - p) % NY, p + 1
        return ((1 - c) * a + c * b) % NY, (c * a + (1 - c) * b) % NY

    def sib_copy(p):
        return remote(sib_out.at[p], sib_in.at[p], sb_s.at[p], sb_r.at[p], sibling)

    def rs_copy(p, d):
        return remote(rsend.at[p, (x + d) % NX], rrecv.at[p, d], rs_s.at[p, d], rs_r.at[p, d], at_x(d))

    def ag_copy(p, d):
        mine, _ = slots(p)
        return remote(gath.at[mine, x], gath.at[mine, x], ag_s.at[p, d], ag_r.at[p, d], at_x(d))

    def relay_copy(p, d):
        mine, _ = slots(p)
        chip = (x + NX - d) % NX
        return remote(gath.at[mine, chip], gath.at[mine, chip], rl_s.at[p, d], rl_r.at[p, d], sibling)

    def yo_copy(k):
        return remote(yout.at[k], yret.at[y], yo_s.at[k], yo_r.at[k], at_y(k))

    def reduce_out(p):
        a, b = (NY - p) % NY, p + 1
        for k in (a, b):
            if k:
                y_copy(NY - k).wait_recv()
        mine, other = slots(p)
        pair = jnp.concatenate([yrecv[other], yrecv[mine]], axis=0)
        pre = dot(pair, w_ref[...])
        sib_out[p] = pre[:BLOCK]
        sib_copy(p).start()
        sib_copy(p).wait_recv()
        total = pre[BLOCK:] + sib_in[p]
        for i in range(NX):
            part = total[:, i * LANE : (i + 1) * LANE]
            rsum[p, i] = part
            rsend[p, i] = part.astype(BF)
        for d in range(1, NX):
            rs_copy(p, d).start()

    def activate_share(p):
        for d in range(1, NX):
            rs_copy(p, d).wait_recv()
        mine, _ = slots(p)
        pre = rsum[p, x]
        for d in range(1, NX):
            pre = pre + rrecv[p, d].astype(F32)
        gate_pre, up_pre = pre[:, :HALF], pre[:, HALF:]
        hidden_part = yrecv[mine, :, ROW - LANE : ROW].astype(F32)[:, HALF:]
        s = 1.0 / (1.0 + jnp.exp(-gate_pre))
        grad_up = hidden_part * (gate_pre * s)
        grad_gate = hidden_part * up_pre * (s * (1.0 + gate_pre * (1.0 - s)))
        gath[mine, x] = jnp.concatenate([grad_gate, grad_up], axis=1).astype(BF)
        relay_copy(p, 0).start()
        for d in range(1, NX):
            ag_copy(p, d).start()

    def rows_back(p):
        for d in range(1, NX):
            ag_copy(p, d).wait_recv()
            relay_copy(p, d).start()
        for d in range(NX):
            relay_copy(p, d).wait_recv()
        a, b = (NY - p) % NY, p + 1
        both = [jnp.concatenate([gath[k, i] for i in range(NX)], axis=1) for k in (a, b)]
        back = dot(jnp.concatenate(both, axis=0), w_ref[...], (((1,), (1,)), ((), ()))).astype(BF)
        for i, k in enumerate((a, b)):
            if k:
                yout[k] = back[i * BLOCK : (i + 1) * BLOCK]
                yo_copy(k).start()
            else:
                yret[y] = back[i * BLOCK : (i + 1) * BLOCK]

    reduce_out(0)
    reduce_out(1)
    activate_share(0)
    reduce_out(2)
    activate_share(1)
    reduce_out(3)
    activate_share(2)
    rows_back(0)
    activate_share(3)
    rows_back(1)
    rows_back(2)
    rows_back(3)

    rows_x = yrecv[...].reshape(NY * BLOCK, ROW)
    for i in range(NX // 2):
        pair = jnp.concatenate([gath[:, 2 * i].reshape(NY * BLOCK, LANE), gath[:, 2 * i + 1].reshape(NY * BLOCK, LANE)], axis=1)
        both = dot(rows_x, pair, (((0,), (0,)), ((), ())))[:FEAT]
        first, second = both[:, :LANE], both[:, LANE:]
        gg_ref[:, i * LANE : (i + 1) * LANE] = jnp.concatenate([first[:, :HALF], second[:, :HALF]], axis=1)
        ug_ref[:, i * LANE : (i + 1) * LANE] = jnp.concatenate([first[:, HALF:], second[:, HALF:]], axis=1)

    for k in range(1, NY):
        yo_copy(k).wait_recv()
    sums = []
    for h in range(HALVES):
        acc = yret[h * GROUP].astype(F32)
        for g in range(1, GROUP):
            acc = acc + yret[h * GROUP + g].astype(F32)
        sums.append(acc.astype(BF))
    spread_i = iota((NZ * ZROWS, HALVES * BLOCK), 0)
    from_i = iota((NZ * ZROWS, HALVES * BLOCK), 1)
    spread_r = spread_i % SLOT
    spread_h = (spread_i % ZROWS) // SLOT
    spread = (
        (from_i == spread_h * BLOCK + (spread_i // ZROWS) * CAP + spread_r) & (spread_r < CAP)
    ).astype(BF)
    back_rows = dot(spread, jnp.concatenate(sums, axis=0)).astype(BF)
    for zz in range(NZ):
        zout[zz] = back_rows[zz * ZROWS : (zz + 1) * ZROWS]

    def zo_copy(d):
        return remote(zout.at[(z + d) % NZ], zret.at[z], zo_s.at[d], zo_r.at[d], at_z(d))

    for d in range(1, NZ):
        zo_copy(d).start()
    zret[z] = zout[z]
    for d in range(1, NZ):
        zo_copy(d).wait_recv()
    got = zret[...].reshape(NZ * ZROWS, ROW)
    mine_back = dot(select, got, (((0,), (0,)), ((), ())))
    tg_ref[...] = mine_back[:, :FEAT].astype(BF)

    for d in range(1, NZ):
        z_copy(d).wait_send()
        zo_copy(d).wait_send()
    for d in range(1, NY):
        y_copy(d).wait_send()
        yo_copy(d).wait_send()
    for p in range(PAIRS):
        sib_copy(p).wait_send()
        relay_copy(p, 0).wait_send()
        for d in range(1, NX):
            rs_copy(p, d).wait_send()
            ag_copy(p, d).wait_send()
            relay_copy(p, d).wait_send()


def shards(tokens, route_expert, hidden_grad, gate_weight, up_weight):
    vmem = pl.BlockSpec(memory_space=pltpu.VMEM)
    dma = pltpu.SemaphoreType.DMA
    return pl.pallas_call(
        kernel,
        out_shape=(
            jax.ShapeDtypeStruct(tokens.shape, BF),
            jax.ShapeDtypeStruct(gate_weight.shape, F32),
            jax.ShapeDtypeStruct(up_weight.shape, F32),
        ),
        in_specs=[vmem] * 5,
        out_specs=(vmem, vmem, vmem),
        scratch_shapes=[
            pltpu.VMEM((ROW, WIDE), BF),
            pltpu.VMEM((NZ, ZROWS, ZWIDE), BF),
            pltpu.VMEM((NZ, ZROWS, ZWIDE), BF),
            pltpu.VMEM((NY, BLOCK, ROW), BF),
            pltpu.VMEM((NY, BLOCK, ROW), BF),
            pltpu.VMEM((PAIRS, BLOCK, WIDE), F32),
            pltpu.VMEM((PAIRS, BLOCK, WIDE), F32),
            pltpu.VMEM((PAIRS, NX, BLOCK, LANE), F32),
            pltpu.VMEM((PAIRS, NX, BLOCK, LANE), BF),
            pltpu.VMEM((PAIRS, NX, BLOCK, LANE), BF),
            pltpu.VMEM((NY, NX, BLOCK, LANE), BF),
            pltpu.VMEM((NY, BLOCK, ROW), BF),
            pltpu.VMEM((NY, BLOCK, ROW), BF),
            pltpu.VMEM((NZ, ZROWS, ROW), BF),
            pltpu.VMEM((NZ, ZROWS, ROW), BF),
            dma((NZ,)), dma((NZ,)),
            dma((NY,)), dma((NY,)),
            dma((PAIRS,)), dma((PAIRS,)),
            dma((PAIRS, NX)), dma((PAIRS, NX)),
            dma((PAIRS, NX)), dma((PAIRS, NX)),
            dma((PAIRS, NX)), dma((PAIRS, NX)),
            dma((NY,)), dma((NY,)),
            dma((NZ,)), dma((NZ,)),
        ],
        compiler_params=pltpu.CompilerParams(
            collective_id=0, has_side_effects=True, vmem_limit_bytes=56 * 1024 * 1024
        ),
    )(route_expert.reshape(1, -1), tokens, hidden_grad, gate_weight, up_weight)


def solution(mesh):
    in_specs = (
        P("node", "local"),
        P("node"),
        P("node", None),
        P("local", "node"),
        P("local", "node"),
    )
    out_specs = (P("node", "local"), P("local", "node"), P("local", "node"))
    return jax.shard_map(shards, mesh=mesh, in_specs=in_specs, out_specs=out_specs, check_vma=False)
```

```python
import functools

import jax
import jax.numpy as jnp
from jax import lax
from jax.experimental import pallas as pl
from jax.experimental.pallas import tpu as pltpu
from jax.sharding import PartitionSpec as P

MESH = pl.DeviceIdType.MESH
BF = jnp.bfloat16
F32 = jnp.float32

NZ, NY, NX = 8, 8, 8
GROUP = 4
HALVES = NY // GROUP
CAP = 10
FEAT = 448
ROW = 512
HALF = 64
LANE = 128
BLOCK = NZ * CAP
SHARE = HALVES * CAP
IN_ROWS = 112
OUT_ROWS = 4 * SHARE
WIDE = NX * LANE
PAIR = ((0, 4), (5, 3), (6, 2), (7, 1))
PAIRS = len(PAIR)
EXPERTS = NZ * HALVES


def iota(shape, dim):
    return lax.broadcasted_iota(jnp.int32, shape, dim)


def dot(a, b, dims=(((1,), (0,)), ((), ()))):
    return lax.dot_general(a, b, dims, preferred_element_type=F32)


def kernel(
    route_any, tok_any, hid_any, gw_any, uw_any,
    tg_ref, gg_any, ug_any,
    route_ref, tok_ref, hid_ref, gw_ref, uw_ref, gg_ref, ug_ref, compact, spread, pick,
    w_ref, zsend, zrecv, ysend, yrecv, sib_out, sib_in, rsum, rsend, rrecv, gath, yout, yret, zout, zret, in_s,
    zs_s, zs_r, ys_s, ys_r, sb_s, sb_r, rs_s, rs_r, ag_s, ag_r, rl_s, rl_r, yo_s, yo_r, zo_s, zo_r,
):
    node, local = lax.axis_index("node"), lax.axis_index("local")
    z, y = node // NY, node % NY
    x, c = local // 2, local % 2

    def at_z(d):
        return (((z + d) % NZ) * NY + y, local)

    def at_y(d):
        return (z * NY + (y + d) % NY, local)

    def at_x(d):
        return (node, ((x + d) % NX) * 2 + c)

    sibling = (node, x * 2 + 1 - c)

    def remote(src, dst, s_sem, r_sem, device):
        return pltpu.make_async_remote_copy(
            src_ref=src, dst_ref=dst, send_sem=s_sem, recv_sem=r_sem, device_id=device, device_id_type=MESH
        )

    odd = x % 2
    loads = [
        pltpu.make_async_copy(route_any, route_ref, in_s.at[0]),
        pltpu.make_async_copy(tok_any, tok_ref.at[0:FEAT], in_s.at[1]),
        pltpu.make_async_copy(gw_any, gw_ref, in_s.at[2]),
        pltpu.make_async_copy(uw_any, uw_ref, in_s.at[3]),
    ]
    for g in range(GROUP):
        start = pl.multiple_of(g * (NX * HALF) + (x // 2) * LANE, LANE)
        loads.append(pltpu.make_async_copy(hid_any.at[:, pl.ds(start, LANE)], hid_ref.at[g], in_s.at[4 + g]))
    for i in (0, 1, 4, 5, 6, 7, 2, 3):
        loads[i].start()

    barrier = pltpu.get_barrier_semaphore()
    for d in range(1, NZ):
        pl.semaphore_signal(barrier, inc=1, device_id=at_z(d), device_id_type=MESH)
    for d in range(1, NY):
        pl.semaphore_signal(barrier, inc=1, device_id=at_y(d), device_id_type=MESH)
    for d in range(1, NX):
        pl.semaphore_signal(barrier, inc=1, device_id=at_x(d), device_id_type=MESH)
    pl.semaphore_signal(barrier, inc=1, device_id=sibling, device_id_type=MESH)

    tok_count = tok_ref.shape[1]
    tok_ref[FEAT:ROW, :] = jnp.zeros((ROW - FEAT, tok_count), BF)
    before = (iota((tok_count, tok_count), 0) < iota((tok_count, tok_count), 1)).astype(BF)
    lane = iota((LANE, LANE), 1)
    shifted = iota((LANE, LANE), 0) - HALF * odd
    place_low = ((shifted == lane) & (lane < HALF)).astype(BF)
    place_high = ((shifted == lane - HALF) & (lane >= HALF)).astype(BF)
    loads[0].wait()
    route = route_ref[...]
    onehot = (iota((EXPERTS, tok_count), 0) == route).astype(F32)
    prior = dot(onehot.astype(BF), before)
    rank = jnp.sum(prior * onehot, axis=0, keepdims=True).astype(jnp.int32)
    to_z, to_h = route // HALVES, route % HALVES
    in_row = iota((NZ * IN_ROWS, tok_count), 0)
    first = to_z * IN_ROWS + to_h * CAP + rank
    last = to_z * IN_ROWS + 5 * SHARE + rank

    loads[1].wait()
    by_lane = (((1,), (1,)), ((), ()))
    packed = jnp.zeros((NZ * IN_ROWS, LANE), F32)
    for j in range(4):
        packed = packed + dot((in_row == first + j * SHARE).astype(BF), tok_ref[j * LANE : (j + 1) * LANE, :], by_lane)
    for g in range(GROUP):
        loads[4 + g].wait()
    hidden_0 = dot(hid_ref[0], place_high).astype(BF)
    hidden_12 = (dot(hid_ref[1], place_low) + dot(hid_ref[2], place_high)).astype(BF)
    hidden_3 = [dot(hid_ref[3], place).astype(BF) for place in (place_low, place_high)]
    packed = packed + dot((in_row == first + 3 * SHARE).astype(BF), hidden_0)
    packed = packed + dot((in_row == first + 4 * SHARE).astype(BF), hidden_12)
    for h in range(HALVES):
        packed = packed + dot(((in_row == last) & (to_h == h)).astype(BF), hidden_3[h])
    for zz in range(NZ):
        zsend[zz] = packed[zz * IN_ROWS : (zz + 1) * IN_ROWS].astype(BF)

    pl.semaphore_wait(barrier, (NZ - 1) + (NY - 1) + (NX - 1) + 1)

    def z_copy(d):
        return remote(zsend.at[(z + d) % NZ], zrecv.at[z], zs_s.at[d], zs_r.at[d], at_z(d))

    for d in range(1, NZ):
        z_copy(d).start()
    zrecv[z] = zsend[z]

    loads[2].wait()
    loads[3].wait()
    for i in range(NX // 2):
        g_part = gw_ref[:, i * LANE : (i + 1) * LANE]
        u_part = uw_ref[:, i * LANE : (i + 1) * LANE]
        w_ref[0:FEAT, 2 * i * LANE : (2 * i + 1) * LANE] = jnp.concatenate([g_part[:, :HALF], u_part[:, :HALF]], axis=1)
        w_ref[0:FEAT, (2 * i + 1) * LANE : (2 * i + 2) * LANE] = jnp.concatenate([g_part[:, HALF:], u_part[:, HALF:]], axis=1)
    w_ref[FEAT:ROW, :] = jnp.zeros((ROW - FEAT, WIDE), BF)

    out_i = iota((HALVES * BLOCK, NZ * IN_ROWS), 0)
    in_i = iota((HALVES * BLOCK, NZ * IN_ROWS), 1)
    start = ((out_i % BLOCK) // CAP) * IN_ROWS + out_i % CAP
    for j in range(5):
        compact[j] = (in_i == start + (out_i // BLOCK) * CAP + j * SHARE).astype(BF)
    compact[5] = (in_i == start + 5 * SHARE).astype(BF)

    out_i = iota((NZ * OUT_ROWS, HALVES * BLOCK), 0)
    in_i = iota((NZ * OUT_ROWS, HALVES * BLOCK), 1)
    start = ((in_i % BLOCK) // CAP) * OUT_ROWS + (in_i // BLOCK) * CAP + in_i % CAP
    out_row = iota((NZ * OUT_ROWS, tok_count), 0)
    for j in range(4):
        spread[j] = (out_i == start + j * SHARE).astype(BF)
        pick[:, j * LANE : (j + 1) * LANE] = (out_row == to_z * OUT_ROWS + to_h * CAP + rank + j * SHARE).astype(BF)

    for d in range(1, NZ):
        z_copy(d).wait_recv()
    rows_in = zrecv[...].reshape(NZ * IN_ROWS, LANE)
    parts = [dot(compact[j], rows_in).astype(BF) for j in range(6)]
    for h in range(HALVES):
        rows = slice(h * BLOCK, (h + 1) * BLOCK)
        features, mixed, middle, final = parts[:3], parts[3][rows], parts[4][rows], parts[5][rows]
        for g in range(GROUP):
            for j in range(3):
                ysend[h * GROUP + g, :, j * LANE : (j + 1) * LANE] = features[j][rows]
            hidden = (mixed[:, HALF:], middle[:, :HALF], middle[:, HALF:], final[:, h * HALF : (h + 1) * HALF])[g]
            ysend[h * GROUP + g, :, ROW - LANE : ROW] = jnp.concatenate([mixed[:, :HALF], hidden], axis=1)

    def y_copy(d):
        return remote(ysend.at[(y + d) % NY], yrecv.at[NY - d], ys_s.at[d], ys_r.at[d], at_y(d))

    y_copy(4).start()
    yrecv[0] = ysend[y]
    y_copy(4).wait_send()
    y_copy(3).start()
    y_copy(5).start()

    def slots(p):
        a, b = PAIR[p]
        return ((1 - c) * a + c * b) % NY, (c * a + (1 - c) * b) % NY

    def sib_copy(p):
        return remote(sib_out.at[p], sib_in.at[p], sb_s.at[p], sb_r.at[p], sibling)

    def rs_copy(p, d):
        return remote(rsend.at[p, (x + d) % NX], rrecv.at[p, d], rs_s.at[p, d], rs_r.at[p, d], at_x(d))

    def ag_copy(p, d):
        mine, _ = slots(p)
        return remote(gath.at[mine, x], gath.at[mine, x], ag_s.at[p, d], ag_r.at[p, d], at_x(d))

    def relay_copy(p, d):
        mine, _ = slots(p)
        chip = (x + NX - d) % NX
        return remote(gath.at[mine, chip], gath.at[mine, chip], rl_s.at[p, d], rl_r.at[p, d], sibling)

    def yo_copy(k):
        return remote(yout.at[k], yret.at[y], yo_s.at[k], yo_r.at[k], at_y(k))

    def next_sends(done, d):
        for k in (done, NY - done):
            y_copy(k).wait_send()
        for k in (d, NY - d):
            y_copy(k).start()

    def pre_part(p):
        for k in PAIR[p]:
            if k:
                y_copy(NY - k).wait_recv()
        mine, other = slots(p)
        pair = jnp.concatenate([yrecv[other], yrecv[mine]], axis=0)
        pre = dot(pair, w_ref[...])
        sib_out[p] = pre[:BLOCK]
        sib_copy(p).start()
        for i in range(NX):
            rsum[p, i] = pre[BLOCK:, i * LANE : (i + 1) * LANE]

    def reduce_near(p):
        sib_copy(p).wait_recv()
        for i in range(NX):
            part = rsum[p, i] + sib_in[p, :, i * LANE : (i + 1) * LANE]
            rsum[p, i] = part
            rsend[p, i] = part.astype(BF)
        for d in range(1, NX):
            rs_copy(p, d).start()

    def rs_wait(p):
        for d in range(1, NX):
            rs_copy(p, d).wait_recv()

    def activate_share(p):
        rs_wait(p)
        mine, _ = slots(p)
        pre = rsum[p, x]
        for d in range(1, NX):
            pre = pre + rrecv[p, d].astype(F32)
        gate_pre, up_pre = pre[:, :HALF], pre[:, HALF:]
        hidden_part = yrecv[mine, :, ROW - LANE : ROW].astype(F32)[:, HALF:]
        s = 1.0 / (1.0 + jnp.exp(-gate_pre))
        grad_up = hidden_part * (gate_pre * s)
        grad_gate = hidden_part * up_pre * (s * (1.0 + gate_pre * (1.0 - s)))
        gath[mine, x] = jnp.concatenate([grad_gate, grad_up], axis=1).astype(BF)
        relay_copy(p, 0).start()
        for d in range(1, NX):
            ag_copy(p, d).start()

    def gather_share(p):
        for d in (1, 7, 2, 6, 3, 5, 4):
            ag_copy(p, d).wait_recv()
            relay_copy(p, d).start()

    def gather_wait(p):
        for d in range(NX):
            relay_copy(p, d).wait_recv()

    def rows_back(p):
        gather_wait(p)
        a, b = PAIR[p]
        both = [jnp.concatenate([gath[k, i] for i in range(NX)], axis=1) for k in (a, b)]
        back = dot(jnp.concatenate(both, axis=0), w_ref[...], (((1,), (1,)), ((), ()))).astype(BF)
        for i, k in enumerate((a, b)):
            if k:
                yout[k] = back[i * BLOCK : (i + 1) * BLOCK]
                yo_copy(k).start()
            else:
                yret[y] = back[i * BLOCK : (i + 1) * BLOCK]

    pre_part(0)
    reduce_near(0)
    next_sends(3, 2)
    pre_part(1)
    reduce_near(1)
    activate_share(0)
    next_sends(2, 1)
    pre_part(2)
    reduce_near(2)
    pre_part(3)
    activate_share(1)
    gather_share(0)
    reduce_near(3)
    rows_back(0)
    activate_share(2)
    gather_share(1)
    activate_share(3)
    rows_back(1)
    gather_share(2)
    rows_back(2)
    gather_share(3)
    rows_back(3)

    for k in range(1, NY):
        yo_copy(k).wait_recv()
    sums = []
    for h in range(HALVES):
        acc = yret[h * GROUP].astype(F32)
        for g in range(1, GROUP):
            acc = acc + yret[h * GROUP + g].astype(F32)
        sums.append(acc.astype(BF))
    total = jnp.concatenate(sums, axis=0)
    back_rows = dot(spread[0], total[:, :LANE])
    for j in range(1, 4):
        back_rows = back_rows + dot(spread[j], total[:, j * LANE : (j + 1) * LANE])
    for zz in range(NZ):
        zout[zz] = back_rows[zz * OUT_ROWS : (zz + 1) * OUT_ROWS].astype(BF)

    def zo_copy(d):
        return remote(zout.at[(z + d) % NZ], zret.at[z], zo_s.at[d], zo_r.at[d], at_z(d))

    for d in range(1, NZ):
        zo_copy(d).start()
    zret[z] = zout[z]

    rows_x = yrecv[...].reshape(NY * BLOCK, ROW)
    for i in range(NX // 2):
        pair = jnp.concatenate([gath[:, 2 * i].reshape(NY * BLOCK, LANE), gath[:, 2 * i + 1].reshape(NY * BLOCK, LANE)], axis=1)
        both = dot(rows_x, pair, (((0,), (0,)), ((), ())))[:FEAT]
        first, second = both[:, :LANE], both[:, LANE:]
        gg_ref[:, i * LANE : (i + 1) * LANE] = jnp.concatenate([first[:, :HALF], second[:, :HALF]], axis=1)
        ug_ref[:, i * LANE : (i + 1) * LANE] = jnp.concatenate([first[:, HALF:], second[:, HALF:]], axis=1)
    stores = [
        pltpu.make_async_copy(gg_ref, gg_any, in_s.at[0]),
        pltpu.make_async_copy(ug_ref, ug_any, in_s.at[1]),
    ]
    for store in stores:
        store.start()

    for d in range(1, NZ):
        zo_copy(d).wait_recv()
    got = zret[...].reshape(NZ * OUT_ROWS, LANE)
    mine_back = dot(got, pick[...], (((0,), (0,)), ((), ()))).astype(BF)
    for j in range(4):
        rows = min(LANE, FEAT - j * LANE)
        tg_ref[j * LANE : j * LANE + rows, :] = mine_back[:rows, j * LANE : (j + 1) * LANE]

    for store in stores:
        store.wait()
    for d in range(1, NZ):
        z_copy(d).wait_send()
        zo_copy(d).wait_send()
    y_copy(1).wait_send()
    y_copy(7).wait_send()
    for d in range(1, NY):
        yo_copy(d).wait_send()
    for p in range(PAIRS):
        sib_copy(p).wait_send()
        relay_copy(p, 0).wait_send()
        for d in range(1, NX):
            rs_copy(p, d).wait_send()
            ag_copy(p, d).wait_send()
            relay_copy(p, d).wait_send()


def shards(tokens, route_expert, hidden_grad, gate_weight, up_weight):
    vmem, anywhere = pl.BlockSpec(memory_space=pltpu.VMEM), pl.BlockSpec(memory_space=pl.ANY)
    tok_count = tokens.shape[0]
    dma = pltpu.SemaphoreType.DMA
    token_grad, gate_grad, up_grad = pl.pallas_call(
        kernel,
        out_shape=(
            jax.ShapeDtypeStruct(tokens.shape[::-1], BF),
            jax.ShapeDtypeStruct(gate_weight.shape, F32),
            jax.ShapeDtypeStruct(up_weight.shape, F32),
        ),
        in_specs=[anywhere] * 5,
        out_specs=(vmem, anywhere, anywhere),
        scratch_shapes=[
            pltpu.VMEM((1, tok_count), jnp.int32),
            pltpu.VMEM((ROW, tok_count), BF),
            pltpu.VMEM((GROUP, tok_count, LANE), BF),
            pltpu.VMEM(gate_weight.shape, BF),
            pltpu.VMEM(up_weight.shape, BF),
            pltpu.VMEM(gate_weight.shape, F32),
            pltpu.VMEM(up_weight.shape, F32),
            pltpu.VMEM((6, HALVES * BLOCK, NZ * IN_ROWS), BF),
            pltpu.VMEM((4, NZ * OUT_ROWS, HALVES * BLOCK), BF),
            pltpu.VMEM((NZ * OUT_ROWS, 4 * tok_count), BF),
            pltpu.VMEM((ROW, WIDE), BF),
            pltpu.VMEM((NZ, IN_ROWS, LANE), BF),
            pltpu.VMEM((NZ, IN_ROWS, LANE), BF),
            pltpu.VMEM((NY, BLOCK, ROW), BF),
            pltpu.VMEM((NY, BLOCK, ROW), BF),
            pltpu.VMEM((PAIRS, BLOCK, WIDE), F32),
            pltpu.VMEM((PAIRS, BLOCK, WIDE), F32),
            pltpu.VMEM((PAIRS, NX, BLOCK, LANE), F32),
            pltpu.VMEM((PAIRS, NX, BLOCK, LANE), BF),
            pltpu.VMEM((PAIRS, NX, BLOCK, LANE), BF),
            pltpu.VMEM((NY, NX, BLOCK, LANE), BF),
            pltpu.VMEM((NY, BLOCK, ROW), BF),
            pltpu.VMEM((NY, BLOCK, ROW), BF),
            pltpu.VMEM((NZ, OUT_ROWS, LANE), BF),
            pltpu.VMEM((NZ, OUT_ROWS, LANE), BF),
            dma((8,)),
            dma((NZ,)), dma((NZ,)),
            dma((NY,)), dma((NY,)),
            dma((PAIRS,)), dma((PAIRS,)),
            dma((PAIRS, NX)), dma((PAIRS, NX)),
            dma((PAIRS, NX)), dma((PAIRS, NX)),
            dma((PAIRS, NX)), dma((PAIRS, NX)),
            dma((NY,)), dma((NY,)),
            dma((NZ,)), dma((NZ,)),
        ],
        compiler_params=pltpu.CompilerParams(
            collective_id=0, has_side_effects=True, vmem_limit_bytes=56 * 1024 * 1024
        ),
    )(route_expert.reshape(1, -1), tokens.T, hidden_grad, gate_weight, up_weight)
    return token_grad.T, gate_grad, up_grad


def solution(mesh):
    in_specs = (
        P("node", "local"),
        P("node"),
        P("node", None),
        P("local", "node"),
        P("local", "node"),
    )
    out_specs = (P("node", "local"), P("local", "node"), P("local", "node"))
    return jax.shard_map(shards, mesh=mesh, in_specs=in_specs, out_specs=out_specs, check_vma=False)
```

```python
import functools

import jax
import jax.numpy as jnp
from jax import lax
from jax.experimental import pallas as pl
from jax.experimental.pallas import tpu as pltpu
from jax.sharding import PartitionSpec as P

MESH = pl.DeviceIdType.MESH
BF = jnp.bfloat16
F32 = jnp.float32

NZ, NY, NX = 8, 8, 8
GROUP = 4
HALVES = NY // GROUP
CAP = 10
FEAT = 448
ROW = 512
HALF = 64
LANE = 128
BLOCK = NZ * CAP
SHARE = HALVES * CAP
IN_ROWS = 112
OUT_ROWS = 4 * SHARE
WIDE = NX * LANE
PAIR = ((0, 4), (5, 3), (6, 2), (7, 1))
PAIRS = len(PAIR)
EXPERTS = NZ * HALVES


def iota(shape, dim):
    return lax.broadcasted_iota(jnp.int32, shape, dim)


def dot(a, b, dims=(((1,), (0,)), ((), ()))):
    return lax.dot_general(a, b, dims, preferred_element_type=F32)


def kernel(
    route_any, tok_any, hid_any, gw_any, uw_any,
    tg_ref, gg_any, ug_any,
    route_ref, tok_ref, hid_ref, gw_ref, uw_ref, gg_ref, ug_ref, compact, spread, pick,
    w_ref, zsend, zrecv, ysend, yrecv, sib_out, sib_in, rsum, rsend, rrecv, gath, yout, yret, zout, zret, in_s,
    zs_s, zs_r, ys_s, ys_r, sb_s, sb_r, rs_s, rs_r, ag_s, ag_r, rl_s, rl_r, yo_s, yo_r, zo_s, zo_r,
):
    node, local = lax.axis_index("node"), lax.axis_index("local")
    z, y = node // NY, node % NY
    x, c = local // 2, local % 2

    def at_z(d):
        return (((z + d) % NZ) * NY + y, local)

    def at_y(d):
        return (z * NY + (y + d) % NY, local)

    def at_x(d):
        return (node, ((x + d) % NX) * 2 + c)

    sibling = (node, x * 2 + 1 - c)

    def remote(src, dst, s_sem, r_sem, device):
        return pltpu.make_async_remote_copy(
            src_ref=src, dst_ref=dst, send_sem=s_sem, recv_sem=r_sem, device_id=device, device_id_type=MESH
        )

    odd = x % 2
    loads = [
        pltpu.make_async_copy(route_any, route_ref, in_s.at[0]),
        pltpu.make_async_copy(tok_any, tok_ref.at[0:FEAT], in_s.at[1]),
        pltpu.make_async_copy(gw_any, gw_ref, in_s.at[2]),
        pltpu.make_async_copy(uw_any, uw_ref, in_s.at[3]),
    ]
    for g in range(GROUP):
        start = pl.multiple_of(g * (NX * HALF) + (x // 2) * LANE, LANE)
        loads.append(pltpu.make_async_copy(hid_any.at[:, pl.ds(start, LANE)], hid_ref.at[g], in_s.at[4 + g]))
    for i in (0, 1, 4, 5, 6, 7, 2, 3):
        loads[i].start()

    barrier = pltpu.get_barrier_semaphore()
    for d in range(1, NZ):
        pl.semaphore_signal(barrier, inc=1, device_id=at_z(d), device_id_type=MESH)
    for d in range(1, NY):
        pl.semaphore_signal(barrier, inc=1, device_id=at_y(d), device_id_type=MESH)
    for d in range(1, NX):
        pl.semaphore_signal(barrier, inc=1, device_id=at_x(d), device_id_type=MESH)
    pl.semaphore_signal(barrier, inc=1, device_id=sibling, device_id_type=MESH)

    tok_count = tok_ref.shape[1]
    tok_ref[FEAT:ROW, :] = jnp.zeros((ROW - FEAT, tok_count), BF)
    before = (iota((tok_count, tok_count), 0) < iota((tok_count, tok_count), 1)).astype(BF)
    lane = iota((LANE, LANE), 1)
    shifted = iota((LANE, LANE), 0) - HALF * odd
    place_low = ((shifted == lane) & (lane < HALF)).astype(BF)
    place_high = ((shifted == lane - HALF) & (lane >= HALF)).astype(BF)
    loads[0].wait()
    route = route_ref[...]
    onehot = (iota((EXPERTS, tok_count), 0) == route).astype(F32)
    prior = dot(onehot.astype(BF), before)
    rank = jnp.sum(prior * onehot, axis=0, keepdims=True).astype(jnp.int32)
    to_z, to_h = route // HALVES, route % HALVES
    in_row = iota((NZ * IN_ROWS, tok_count), 0)
    first = to_z * IN_ROWS + to_h * CAP + rank
    last = to_z * IN_ROWS + 5 * SHARE + rank

    loads[1].wait()
    by_lane = (((1,), (1,)), ((), ()))
    packed = jnp.zeros((NZ * IN_ROWS, LANE), F32)
    for j in range(4):
        packed = packed + dot((in_row == first + j * SHARE).astype(BF), tok_ref[j * LANE : (j + 1) * LANE, :], by_lane)
    for g in range(GROUP):
        loads[4 + g].wait()
    hidden_0 = dot(hid_ref[0], place_high).astype(BF)
    hidden_12 = (dot(hid_ref[1], place_low) + dot(hid_ref[2], place_high)).astype(BF)
    hidden_3 = [dot(hid_ref[3], place).astype(BF) for place in (place_low, place_high)]
    packed = packed + dot((in_row == first + 3 * SHARE).astype(BF), hidden_0)
    packed = packed + dot((in_row == first + 4 * SHARE).astype(BF), hidden_12)
    for h in range(HALVES):
        packed = packed + dot(((in_row == last) & (to_h == h)).astype(BF), hidden_3[h])
    for zz in range(NZ):
        zsend[zz] = packed[zz * IN_ROWS : (zz + 1) * IN_ROWS].astype(BF)

    pl.semaphore_wait(barrier, (NZ - 1) + (NY - 1) + (NX - 1) + 1)

    def z_copy(d):
        return remote(zsend.at[(z + d) % NZ], zrecv.at[z], zs_s.at[d], zs_r.at[d], at_z(d))

    for d in range(1, NZ):
        z_copy(d).start()
    zrecv[z] = zsend[z]

    loads[2].wait()
    loads[3].wait()
    for i in range(NX // 2):
        g_part = gw_ref[:, i * LANE : (i + 1) * LANE]
        u_part = uw_ref[:, i * LANE : (i + 1) * LANE]
        w_ref[0:FEAT, 2 * i * LANE : (2 * i + 1) * LANE] = jnp.concatenate([g_part[:, :HALF], u_part[:, :HALF]], axis=1)
        w_ref[0:FEAT, (2 * i + 1) * LANE : (2 * i + 2) * LANE] = jnp.concatenate([g_part[:, HALF:], u_part[:, HALF:]], axis=1)
    w_ref[FEAT:ROW, :] = jnp.zeros((ROW - FEAT, WIDE), BF)

    out_i = iota((HALVES * BLOCK, NZ * IN_ROWS), 0)
    in_i = iota((HALVES * BLOCK, NZ * IN_ROWS), 1)
    start = ((out_i % BLOCK) // CAP) * IN_ROWS + out_i % CAP
    for j in range(5):
        compact[j] = (in_i == start + (out_i // BLOCK) * CAP + j * SHARE).astype(BF)
    compact[5] = (in_i == start + 5 * SHARE).astype(BF)

    out_i = iota((NZ * OUT_ROWS, HALVES * BLOCK), 0)
    in_i = iota((NZ * OUT_ROWS, HALVES * BLOCK), 1)
    start = ((in_i % BLOCK) // CAP) * OUT_ROWS + (in_i // BLOCK) * CAP + in_i % CAP
    out_row = iota((NZ * OUT_ROWS, tok_count), 0)
    for j in range(4):
        spread[j] = (out_i == start + j * SHARE).astype(BF)
        pick[:, j * LANE : (j + 1) * LANE] = (out_row == to_z * OUT_ROWS + to_h * CAP + rank + j * SHARE).astype(BF)

    for d in range(1, NZ):
        z_copy(d).wait_recv()
    rows_in = zrecv[...].reshape(NZ * IN_ROWS, LANE)
    parts = [dot(compact[j], rows_in).astype(BF) for j in range(6)]
    for h in range(HALVES):
        rows = slice(h * BLOCK, (h + 1) * BLOCK)
        features, mixed, middle, final = parts[:3], parts[3][rows], parts[4][rows], parts[5][rows]
        for g in range(GROUP):
            for j in range(3):
                ysend[h * GROUP + g, :, j * LANE : (j + 1) * LANE] = features[j][rows]
            hidden = (mixed[:, HALF:], middle[:, :HALF], middle[:, HALF:], final[:, h * HALF : (h + 1) * HALF])[g]
            ysend[h * GROUP + g, :, ROW - LANE : ROW] = jnp.concatenate([mixed[:, :HALF], hidden], axis=1)

    def y_copy(d):
        return remote(ysend.at[(y + d) % NY], yrecv.at[NY - d], ys_s.at[d], ys_r.at[d], at_y(d))

    y_copy(4).start()
    yrecv[0] = ysend[y]
    y_copy(4).wait_send()
    y_copy(3).start()
    y_copy(5).start()

    def slots(p):
        a, b = PAIR[p]
        return ((1 - c) * a + c * b) % NY, (c * a + (1 - c) * b) % NY

    def sib_copy(p):
        return remote(sib_out.at[p], sib_in.at[p], sb_s.at[p], sb_r.at[p], sibling)

    def rs_copy(p, d):
        return remote(rsend.at[p, (x + d) % NX], rrecv.at[p, d], rs_s.at[p, d], rs_r.at[p, d], at_x(d))

    def ag_copy(p, d):
        mine, _ = slots(p)
        return remote(gath.at[mine, x], gath.at[mine, x], ag_s.at[p, d], ag_r.at[p, d], at_x(d))

    def relay_copy(p, d):
        mine, _ = slots(p)
        chip = (x + NX - d) % NX
        return remote(gath.at[mine, chip], gath.at[mine, chip], rl_s.at[p, d], rl_r.at[p, d], sibling)

    def yo_copy(k):
        return remote(yout.at[k], yret.at[y], yo_s.at[k], yo_r.at[k], at_y(k))

    def next_sends(done, d):
        for k in (done, NY - done):
            y_copy(k).wait_send()
        for k in (d, NY - d):
            y_copy(k).start()

    def pre_part(p):
        for k in PAIR[p]:
            if k:
                y_copy(NY - k).wait_recv()
        mine, other = slots(p)
        pair = jnp.concatenate([yrecv[other], yrecv[mine]], axis=0)
        pre = dot(pair, w_ref[...])
        sib_out[p] = pre[:BLOCK]
        sib_copy(p).start()
        for i in range(NX):
            rsum[p, i] = pre[BLOCK:, i * LANE : (i + 1) * LANE]

    def reduce_near(p):
        sib_copy(p).wait_recv()
        for i in range(NX):
            part = rsum[p, i] + sib_in[p, :, i * LANE : (i + 1) * LANE]
            rsum[p, i] = part
            rsend[p, i] = part.astype(BF)
        for d in range(1, NX):
            rs_copy(p, d).start()

    def rs_wait(p):
        for d in range(1, NX):
            rs_copy(p, d).wait_recv()

    def activate_share(p):
        rs_wait(p)
        mine, _ = slots(p)
        pre = rsum[p, x]
        for d in range(1, NX):
            pre = pre + rrecv[p, d].astype(F32)
        gate_pre, up_pre = pre[:, :HALF], pre[:, HALF:]
        hidden_part = yrecv[mine, :, ROW - LANE : ROW].astype(F32)[:, HALF:]
        s = 1.0 / (1.0 + jnp.exp(-gate_pre))
        grad_up = hidden_part * (gate_pre * s)
        grad_gate = hidden_part * up_pre * (s * (1.0 + gate_pre * (1.0 - s)))
        gath[mine, x] = jnp.concatenate([grad_gate, grad_up], axis=1).astype(BF)
        relay_copy(p, 0).start()
        for d in range(1, NX):
            ag_copy(p, d).start()

    def gather_share(p):
        for d in (1, 7, 2, 6, 3, 5, 4):
            ag_copy(p, d).wait_recv()
            relay_copy(p, d).start()

    def gather_wait(p):
        for d in range(NX):
            relay_copy(p, d).wait_recv()

    def rows_back(p):
        gather_wait(p)
        a, b = PAIR[p]
        both = [jnp.concatenate([gath[k, i] for i in range(NX)], axis=1) for k in (a, b)]
        back = dot(jnp.concatenate(both, axis=0), w_ref[...], (((1,), (1,)), ((), ()))).astype(BF)
        for i, k in enumerate((a, b)):
            if k:
                yout[k] = back[i * BLOCK : (i + 1) * BLOCK]
                yo_copy(k).start()
            else:
                yret[y] = back[i * BLOCK : (i + 1) * BLOCK]

    pre_part(0)
    reduce_near(0)
    next_sends(3, 2)
    pre_part(1)
    reduce_near(1)
    activate_share(0)
    next_sends(2, 1)
    pre_part(2)
    reduce_near(2)
    pre_part(3)
    activate_share(1)
    gather_share(0)
    reduce_near(3)
    rows_back(0)
    activate_share(2)
    gather_share(1)
    activate_share(3)
    rows_back(1)
    gather_share(2)
    rows_back(2)
    gather_share(3)
    rows_back(3)

    for k in range(1, NY):
        yo_copy(k).wait_recv()
    sums = []
    for h in range(HALVES):
        acc = yret[h * GROUP].astype(F32)
        for g in range(1, GROUP):
            acc = acc + yret[h * GROUP + g].astype(F32)
        sums.append(acc.astype(BF))
    total = jnp.concatenate(sums, axis=0)
    back_rows = dot(spread[0], total[:, :LANE])
    for j in range(1, 4):
        back_rows = back_rows + dot(spread[j], total[:, j * LANE : (j + 1) * LANE])
    for zz in range(NZ):
        zout[zz] = back_rows[zz * OUT_ROWS : (zz + 1) * OUT_ROWS].astype(BF)

    def zo_copy(d):
        return remote(zout.at[(z + d) % NZ], zret.at[z], zo_s.at[d], zo_r.at[d], at_z(d))

    for d in range(1, NZ):
        zo_copy(d).start()
    zret[z] = zout[z]

    rows_x = yrecv[...].reshape(NY * BLOCK, ROW)
    for i in range(NX // 2):
        pair = jnp.concatenate([gath[:, 2 * i].reshape(NY * BLOCK, LANE), gath[:, 2 * i + 1].reshape(NY * BLOCK, LANE)], axis=1)
        both = dot(rows_x, pair, (((0,), (0,)), ((), ())))[:FEAT]
        first, second = both[:, :LANE], both[:, LANE:]
        gg_ref[:, i * LANE : (i + 1) * LANE] = jnp.concatenate([first[:, :HALF], second[:, :HALF]], axis=1)
        ug_ref[:, i * LANE : (i + 1) * LANE] = jnp.concatenate([first[:, HALF:], second[:, HALF:]], axis=1)
    stores = [
        pltpu.make_async_copy(gg_ref, gg_any, in_s.at[0]),
        pltpu.make_async_copy(ug_ref, ug_any, in_s.at[1]),
    ]
    for store in stores:
        store.start()

    for d in range(1, NZ):
        zo_copy(d).wait_recv()
    got = zret[...].reshape(NZ * OUT_ROWS, LANE)
    mine_back = dot(got, pick[...], (((0,), (0,)), ((), ()))).astype(BF)
    for j in range(4):
        rows = min(LANE, FEAT - j * LANE)
        tg_ref[j * LANE : j * LANE + rows, :] = mine_back[:rows, j * LANE : (j + 1) * LANE]

    for store in stores:
        store.wait()
    for d in range(1, NZ):
        z_copy(d).wait_send()
        zo_copy(d).wait_send()
    y_copy(1).wait_send()
    y_copy(7).wait_send()
    for d in range(1, NY):
        yo_copy(d).wait_send()
    for p in range(PAIRS):
        sib_copy(p).wait_send()
        relay_copy(p, 0).wait_send()
        for d in range(1, NX):
            rs_copy(p, d).wait_send()
            ag_copy(p, d).wait_send()
            relay_copy(p, d).wait_send()


def hand_over(arrays):
    cuts = [(i, part) for i, array in enumerate(arrays) for part in range(array.shape[0] // 112)]

    def body(*refs):
        count = len(arrays)
        ins, outs, held = refs[:count], refs[count : 2 * count], refs[2 * count : 3 * count]
        in_sems, out_sems = refs[3 * count :]
        loads, stores = [], []
        for n, (i, part) in enumerate(cuts):
            rows = pl.ds(part * 112, 112)
            loads.append(pltpu.make_async_copy(ins[i].at[rows], held[i].at[rows], in_sems.at[n]))
            stores.append(pltpu.make_async_copy(held[i].at[rows], outs[i].at[rows], out_sems.at[n]))
        for load in loads:
            load.start()
        for load, store in zip(loads, stores):
            load.wait()
            store.start()
        for store in stores:
            store.wait()

    anywhere = pl.BlockSpec(memory_space=pl.ANY)
    return pl.pallas_call(
        body,
        out_shape=tuple(jax.ShapeDtypeStruct(array.shape, array.dtype) for array in arrays),
        in_specs=[anywhere] * len(arrays),
        out_specs=(anywhere,) * len(arrays),
        scratch_shapes=[pltpu.VMEM(array.shape, array.dtype) for array in arrays]
        + [pltpu.SemaphoreType.DMA((len(cuts),))] * 2,
    )(*arrays)


def shards(tokens, route_expert, hidden_grad, gate_weight, up_weight):
    vmem, anywhere = pl.BlockSpec(memory_space=pltpu.VMEM), pl.BlockSpec(memory_space=pl.ANY)
    tok_count = tokens.shape[0]
    dma = pltpu.SemaphoreType.DMA
    token_grad, gate_grad, up_grad = pl.pallas_call(
        kernel,
        out_shape=(
            jax.ShapeDtypeStruct(tokens.shape[::-1], BF),
            jax.ShapeDtypeStruct(gate_weight.shape, F32),
            jax.ShapeDtypeStruct(up_weight.shape, F32),
        ),
        in_specs=[anywhere] * 5,
        out_specs=(vmem, anywhere, anywhere),
        scratch_shapes=[
            pltpu.VMEM((1, tok_count), jnp.int32),
            pltpu.VMEM((ROW, tok_count), BF),
            pltpu.VMEM((GROUP, tok_count, LANE), BF),
            pltpu.VMEM(gate_weight.shape, BF),
            pltpu.VMEM(up_weight.shape, BF),
            pltpu.VMEM(gate_weight.shape, F32),
            pltpu.VMEM(up_weight.shape, F32),
            pltpu.VMEM((6, HALVES * BLOCK, NZ * IN_ROWS), BF),
            pltpu.VMEM((4, NZ * OUT_ROWS, HALVES * BLOCK), BF),
            pltpu.VMEM((NZ * OUT_ROWS, 4 * tok_count), BF),
            pltpu.VMEM((ROW, WIDE), BF),
            pltpu.VMEM((NZ, IN_ROWS, LANE), BF),
            pltpu.VMEM((NZ, IN_ROWS, LANE), BF),
            pltpu.VMEM((NY, BLOCK, ROW), BF),
            pltpu.VMEM((NY, BLOCK, ROW), BF),
            pltpu.VMEM((PAIRS, BLOCK, WIDE), F32),
            pltpu.VMEM((PAIRS, BLOCK, WIDE), F32),
            pltpu.VMEM((PAIRS, NX, BLOCK, LANE), F32),
            pltpu.VMEM((PAIRS, NX, BLOCK, LANE), BF),
            pltpu.VMEM((PAIRS, NX, BLOCK, LANE), BF),
            pltpu.VMEM((NY, NX, BLOCK, LANE), BF),
            pltpu.VMEM((NY, BLOCK, ROW), BF),
            pltpu.VMEM((NY, BLOCK, ROW), BF),
            pltpu.VMEM((NZ, OUT_ROWS, LANE), BF),
            pltpu.VMEM((NZ, OUT_ROWS, LANE), BF),
            dma((8,)),
            dma((NZ,)), dma((NZ,)),
            dma((NY,)), dma((NY,)),
            dma((PAIRS,)), dma((PAIRS,)),
            dma((PAIRS, NX)), dma((PAIRS, NX)),
            dma((PAIRS, NX)), dma((PAIRS, NX)),
            dma((PAIRS, NX)), dma((PAIRS, NX)),
            dma((NY,)), dma((NY,)),
            dma((NZ,)), dma((NZ,)),
        ],
        compiler_params=pltpu.CompilerParams(
            collective_id=0, has_side_effects=True, vmem_limit_bytes=56 * 1024 * 1024
        ),
    )(route_expert.reshape(1, -1), tokens.T, hidden_grad, gate_weight, up_weight)
    token_grad, gate_grad, up_grad = hand_over((token_grad, gate_grad, up_grad))
    return token_grad.T, gate_grad, up_grad


def solution(mesh):
    in_specs = (
        P("node", "local"),
        P("node"),
        P("node", None),
        P("local", "node"),
        P("local", "node"),
    )
    out_specs = (P("node", "local"), P("local", "node"), P("local", "node"))
    return jax.shard_map(shards, mesh=mesh, in_specs=in_specs, out_specs=out_specs, check_vma=False)
```

```python
import functools

import jax
import jax.numpy as jnp
from jax import lax
from jax.experimental import pallas as pl
from jax.experimental.pallas import tpu as pltpu
from jax.sharding import PartitionSpec as P

MESH = pl.DeviceIdType.MESH
BF = jnp.bfloat16
F32 = jnp.float32

NZ, NY, NX = 8, 8, 8
GROUP = 4
HALVES = NY // GROUP
CAP = 10
FEAT = 448
ROW = 512
HALF = 64
LANE = 128
BLOCK = NZ * CAP
SHARE = HALVES * CAP
IN_ROWS = 112
OUT_ROWS = 4 * SHARE
WIDE = NX * LANE
PAIR = ((0, 4), (5, 3), (6, 2), (7, 1))
PAIRS = len(PAIR)
EXPERTS = NZ * HALVES


def iota(shape, dim):
    return lax.broadcasted_iota(jnp.int32, shape, dim)


def dot(a, b, dims=(((1,), (0,)), ((), ()))):
    return lax.dot_general(a, b, dims, preferred_element_type=F32)


def kernel(
    route_any, tok_any, hid_any, gw_any, uw_any,
    tg_ref, gg_any, ug_any,
    route_ref, tok_ref, hid_ref, gw_ref, uw_ref, gg_ref, ug_ref, compact, spread, pick,
    w_ref, zsend, zrecv, ysend, yrecv, sib_out, sib_in, rsum, rsend, rrecv, gath, yout, yret, zout, zret, in_s,
    zs_s, zs_r, ys_s, ys_r, sb_s, sb_r, rs_s, rs_r, ag_s, ag_r, rl_s, rl_r, yo_s, yo_r, zo_s, zo_r,
):
    node, local = lax.axis_index("node"), lax.axis_index("local")
    z, y = node // NY, node % NY
    x, c = local // 2, local % 2

    def at_z(d):
        return (((z + d) % NZ) * NY + y, local)

    def at_y(d):
        return (z * NY + (y + d) % NY, local)

    def at_x(d):
        return (node, ((x + d) % NX) * 2 + c)

    sibling = (node, x * 2 + 1 - c)

    def remote(src, dst, s_sem, r_sem, device):
        return pltpu.make_async_remote_copy(
            src_ref=src, dst_ref=dst, send_sem=s_sem, recv_sem=r_sem, device_id=device, device_id_type=MESH
        )

    odd = x % 2
    loads = [
        pltpu.make_async_copy(route_any, route_ref, in_s.at[0]),
        pltpu.make_async_copy(tok_any, tok_ref.at[0:FEAT], in_s.at[1]),
        pltpu.make_async_copy(gw_any, gw_ref, in_s.at[2]),
        pltpu.make_async_copy(uw_any, uw_ref, in_s.at[3]),
    ]
    for g in range(GROUP):
        start = pl.multiple_of(g * (NX * HALF) + (x // 2) * LANE, LANE)
        loads.append(pltpu.make_async_copy(hid_any.at[:, pl.ds(start, LANE)], hid_ref.at[g], in_s.at[4 + g]))
    for i in (0, 1, 4, 5, 6, 7, 2, 3):
        loads[i].start()

    barrier = pltpu.get_barrier_semaphore()
    for d in range(1, NZ):
        pl.semaphore_signal(barrier, inc=1, device_id=at_z(d), device_id_type=MESH)
    for d in range(1, NY):
        pl.semaphore_signal(barrier, inc=1, device_id=at_y(d), device_id_type=MESH)
    for d in range(1, NX):
        pl.semaphore_signal(barrier, inc=1, device_id=at_x(d), device_id_type=MESH)
    pl.semaphore_signal(barrier, inc=1, device_id=sibling, device_id_type=MESH)

    tok_count = tok_ref.shape[1]
    tok_ref[FEAT:ROW, :] = jnp.zeros((ROW - FEAT, tok_count), BF)
    before = (iota((tok_count, tok_count), 0) < iota((tok_count, tok_count), 1)).astype(BF)
    lane = iota((LANE, LANE), 1)
    shifted = iota((LANE, LANE), 0) - HALF * odd
    place_low = ((shifted == lane) & (lane < HALF)).astype(BF)
    place_high = ((shifted == lane - HALF) & (lane >= HALF)).astype(BF)
    loads[0].wait()
    route = route_ref[...]
    onehot = (iota((EXPERTS, tok_count), 0) == route).astype(F32)
    prior = dot(onehot.astype(BF), before)
    rank = jnp.sum(prior * onehot, axis=0, keepdims=True).astype(jnp.int32)
    to_z, to_h = route // HALVES, route % HALVES
    in_row = iota((NZ * IN_ROWS, tok_count), 0)
    first = to_z * IN_ROWS + to_h * CAP + rank
    last = to_z * IN_ROWS + 5 * SHARE + rank

    loads[1].wait()
    by_lane = (((1,), (1,)), ((), ()))
    packed = jnp.zeros((NZ * IN_ROWS, LANE), F32)
    for j in range(4):
        packed = packed + dot((in_row == first + j * SHARE).astype(BF), tok_ref[j * LANE : (j + 1) * LANE, :], by_lane)
    for g in range(GROUP):
        loads[4 + g].wait()
    hidden_0 = dot(hid_ref[0], place_high).astype(BF)
    hidden_12 = (dot(hid_ref[1], place_low) + dot(hid_ref[2], place_high)).astype(BF)
    hidden_3 = [dot(hid_ref[3], place).astype(BF) for place in (place_low, place_high)]
    packed = packed + dot((in_row == first + 3 * SHARE).astype(BF), hidden_0)
    packed = packed + dot((in_row == first + 4 * SHARE).astype(BF), hidden_12)
    for h in range(HALVES):
        packed = packed + dot(((in_row == last) & (to_h == h)).astype(BF), hidden_3[h])
    for zz in range(NZ):
        zsend[zz] = packed[zz * IN_ROWS : (zz + 1) * IN_ROWS].astype(BF)

    pl.semaphore_wait(barrier, (NZ - 1) + (NY - 1) + (NX - 1) + 1)

    def z_copy(d):
        return remote(zsend.at[(z + d) % NZ], zrecv.at[z], zs_s.at[d], zs_r.at[d], at_z(d))

    for d in range(1, NZ):
        z_copy(d).start()
    zrecv[z] = zsend[z]

    loads[2].wait()
    loads[3].wait()
    for i in range(NX // 2):
        g_part = gw_ref[:, i * LANE : (i + 1) * LANE]
        u_part = uw_ref[:, i * LANE : (i + 1) * LANE]
        w_ref[0:FEAT, 2 * i * LANE : (2 * i + 1) * LANE] = jnp.concatenate([g_part[:, :HALF], u_part[:, :HALF]], axis=1)
        w_ref[0:FEAT, (2 * i + 1) * LANE : (2 * i + 2) * LANE] = jnp.concatenate([g_part[:, HALF:], u_part[:, HALF:]], axis=1)
    w_ref[FEAT:ROW, :] = jnp.zeros((ROW - FEAT, WIDE), BF)

    out_i = iota((HALVES * BLOCK, NZ * IN_ROWS), 0)
    in_i = iota((HALVES * BLOCK, NZ * IN_ROWS), 1)
    start = ((out_i % BLOCK) // CAP) * IN_ROWS + out_i % CAP
    for j in range(5):
        compact[j] = (in_i == start + (out_i // BLOCK) * CAP + j * SHARE).astype(BF)
    compact[5] = (in_i == start + 5 * SHARE).astype(BF)

    out_i = iota((NZ * OUT_ROWS, HALVES * BLOCK), 0)
    in_i = iota((NZ * OUT_ROWS, HALVES * BLOCK), 1)
    start = ((in_i % BLOCK) // CAP) * OUT_ROWS + (in_i // BLOCK) * CAP + in_i % CAP
    out_row = iota((NZ * OUT_ROWS, tok_count), 0)
    for j in range(4):
        spread[j] = (out_i == start + j * SHARE).astype(BF)
        pick[:, j * LANE : (j + 1) * LANE] = (out_row == to_z * OUT_ROWS + to_h * CAP + rank + j * SHARE).astype(BF)

    for d in range(1, NZ):
        z_copy(d).wait_recv()
    rows_in = zrecv[...].reshape(NZ * IN_ROWS, LANE)
    parts = [dot(compact[j], rows_in).astype(BF) for j in range(6)]
    for h in range(HALVES):
        rows = slice(h * BLOCK, (h + 1) * BLOCK)
        features, mixed, middle, final = parts[:3], parts[3][rows], parts[4][rows], parts[5][rows]
        for g in range(GROUP):
            for j in range(3):
                ysend[h * GROUP + g, :, j * LANE : (j + 1) * LANE] = features[j][rows]
            hidden = (mixed[:, HALF:], middle[:, :HALF], middle[:, HALF:], final[:, h * HALF : (h + 1) * HALF])[g]
            ysend[h * GROUP + g, :, ROW - LANE : ROW] = jnp.concatenate([mixed[:, :HALF], hidden], axis=1)

    def y_copy(d):
        return remote(ysend.at[(y + d) % NY], yrecv.at[NY - d], ys_s.at[d], ys_r.at[d], at_y(d))

    y_copy(4).start()
    yrecv[0] = ysend[y]
    y_copy(4).wait_send()
    y_copy(3).start()
    y_copy(5).start()

    def slots(p):
        a, b = PAIR[p]
        return ((1 - c) * a + c * b) % NY, (c * a + (1 - c) * b) % NY

    def sib_copy(p):
        return remote(sib_out.at[p], sib_in.at[p], sb_s.at[p], sb_r.at[p], sibling)

    def rs_copy(p, d):
        return remote(rsend.at[p, (x + d) % NX], rrecv.at[p, d], rs_s.at[p, d], rs_r.at[p, d], at_x(d))

    def ag_copy(p, d):
        mine, _ = slots(p)
        return remote(gath.at[mine, x], gath.at[mine, x], ag_s.at[p, d], ag_r.at[p, d], at_x(d))

    def relay_copy(p, d):
        mine, _ = slots(p)
        chip = (x + NX - d) % NX
        return remote(gath.at[mine, chip], gath.at[mine, chip], rl_s.at[p, d], rl_r.at[p, d], sibling)

    def yo_copy(k):
        return remote(yout.at[k], yret.at[y], yo_s.at[k], yo_r.at[k], at_y(k))

    def next_sends(done, d):
        for k in (done, NY - done):
            y_copy(k).wait_send()
        for k in (d, NY - d):
            y_copy(k).start()

    def pre_part(p):
        for k in PAIR[p]:
            if k:
                y_copy(NY - k).wait_recv()
        mine, other = slots(p)
        sib_out[p] = dot(yrecv[other], w_ref[...])
        sib_copy(p).start()
        pre = dot(yrecv[mine], w_ref[...])
        for i in range(NX):
            rsum[p, i] = pre[:, i * LANE : (i + 1) * LANE]

    def reduce_near(p):
        sib_copy(p).wait_recv()
        for i in range(NX):
            part = rsum[p, i] + sib_in[p, :, i * LANE : (i + 1) * LANE]
            rsum[p, i] = part
            rsend[p, i] = part.astype(BF)
        for d in range(1, NX):
            rs_copy(p, d).start()

    def rs_wait(p):
        for d in range(1, NX):
            rs_copy(p, d).wait_recv()

    def activate_share(p):
        rs_wait(p)
        mine, _ = slots(p)
        pre = rsum[p, x]
        for d in range(1, NX):
            pre = pre + rrecv[p, d].astype(F32)
        gate_pre, up_pre = pre[:, :HALF], pre[:, HALF:]
        hidden_part = yrecv[mine, :, ROW - LANE : ROW].astype(F32)[:, HALF:]
        s = 1.0 / (1.0 + jnp.exp(-gate_pre))
        grad_up = hidden_part * (gate_pre * s)
        grad_gate = hidden_part * up_pre * (s * (1.0 + gate_pre * (1.0 - s)))
        gath[mine, x] = jnp.concatenate([grad_gate, grad_up], axis=1).astype(BF)
        relay_copy(p, 0).start()
        for d in range(1, NX):
            ag_copy(p, d).start()

    def gather_share(p):
        for d in (1, 7, 2, 6, 3, 5, 4):
            ag_copy(p, d).wait_recv()
            relay_copy(p, d).start()

    def gather_wait(p):
        for d in range(NX):
            relay_copy(p, d).wait_recv()

    def rows_back(p):
        gather_wait(p)
        a, b = PAIR[p]
        both = [jnp.concatenate([gath[k, i] for i in range(NX)], axis=1) for k in (a, b)]
        back = dot(jnp.concatenate(both, axis=0), w_ref[...], (((1,), (1,)), ((), ()))).astype(BF)
        for i, k in enumerate((a, b)):
            if k:
                yout[k] = back[i * BLOCK : (i + 1) * BLOCK]
                yo_copy(k).start()
            else:
                yret[y] = back[i * BLOCK : (i + 1) * BLOCK]

    pre_part(0)
    reduce_near(0)
    next_sends(3, 2)
    pre_part(1)
    reduce_near(1)
    activate_share(0)
    next_sends(2, 1)
    pre_part(2)
    reduce_near(2)
    pre_part(3)
    activate_share(1)
    gather_share(0)
    reduce_near(3)
    rows_back(0)
    activate_share(2)
    gather_share(1)
    activate_share(3)
    rows_back(1)
    gather_share(2)
    rows_back(2)
    gather_share(3)
    rows_back(3)

    for k in range(1, NY):
        yo_copy(k).wait_recv()
    sums = []
    for h in range(HALVES):
        acc = yret[h * GROUP].astype(F32)
        for g in range(1, GROUP):
            acc = acc + yret[h * GROUP + g].astype(F32)
        sums.append(acc.astype(BF))
    total = jnp.concatenate(sums, axis=0)
    back_rows = dot(spread[0], total[:, :LANE])
    for j in range(1, 4):
        back_rows = back_rows + dot(spread[j], total[:, j * LANE : (j + 1) * LANE])
    for zz in range(NZ):
        zout[zz] = back_rows[zz * OUT_ROWS : (zz + 1) * OUT_ROWS].astype(BF)

    def zo_copy(d):
        return remote(zout.at[(z + d) % NZ], zret.at[z], zo_s.at[d], zo_r.at[d], at_z(d))

    for d in range(1, NZ):
        zo_copy(d).start()
    zret[z] = zout[z]

    rows_x = yrecv[...].reshape(NY * BLOCK, ROW)
    for i in range(NX // 2):
        pair = jnp.concatenate([gath[:, 2 * i].reshape(NY * BLOCK, LANE), gath[:, 2 * i + 1].reshape(NY * BLOCK, LANE)], axis=1)
        both = dot(rows_x, pair, (((0,), (0,)), ((), ())))[:FEAT]
        first, second = both[:, :LANE], both[:, LANE:]
        gg_ref[:, i * LANE : (i + 1) * LANE] = jnp.concatenate([first[:, :HALF], second[:, :HALF]], axis=1)
        ug_ref[:, i * LANE : (i + 1) * LANE] = jnp.concatenate([first[:, HALF:], second[:, HALF:]], axis=1)
    stores = [
        pltpu.make_async_copy(gg_ref, gg_any, in_s.at[0]),
        pltpu.make_async_copy(ug_ref, ug_any, in_s.at[1]),
    ]
    for store in stores:
        store.start()

    for d in range(1, NZ):
        zo_copy(d).wait_recv()
    got = zret[...].reshape(NZ * OUT_ROWS, LANE)
    mine_back = dot(got, pick[...], (((0,), (0,)), ((), ()))).astype(BF)
    for j in range(4):
        rows = min(LANE, FEAT - j * LANE)
        tg_ref[j * LANE : j * LANE + rows, :] = mine_back[:rows, j * LANE : (j + 1) * LANE]

    for store in stores:
        store.wait()
    for d in range(1, NZ):
        z_copy(d).wait_send()
        zo_copy(d).wait_send()
    y_copy(1).wait_send()
    y_copy(7).wait_send()
    for d in range(1, NY):
        yo_copy(d).wait_send()
    for p in range(PAIRS):
        sib_copy(p).wait_send()
        relay_copy(p, 0).wait_send()
        for d in range(1, NX):
            rs_copy(p, d).wait_send()
            ag_copy(p, d).wait_send()
            relay_copy(p, d).wait_send()


def hand_over(arrays):
    cuts = [(i, part) for i, array in enumerate(arrays) for part in range(array.shape[0] // 112)]

    def body(*refs):
        count = len(arrays)
        ins, outs, held = refs[:count], refs[count : 2 * count], refs[2 * count : 3 * count]
        in_sems, out_sems = refs[3 * count :]
        loads, stores = [], []
        for n, (i, part) in enumerate(cuts):
            rows = pl.ds(part * 112, 112)
            loads.append(pltpu.make_async_copy(ins[i].at[rows], held[i].at[rows], in_sems.at[n]))
            stores.append(pltpu.make_async_copy(held[i].at[rows], outs[i].at[rows], out_sems.at[n]))
        for load in loads:
            load.start()
        for load, store in zip(loads, stores):
            load.wait()
            store.start()
        for store in stores:
            store.wait()

    anywhere = pl.BlockSpec(memory_space=pl.ANY)
    return pl.pallas_call(
        body,
        out_shape=tuple(jax.ShapeDtypeStruct(array.shape, array.dtype) for array in arrays),
        in_specs=[anywhere] * len(arrays),
        out_specs=(anywhere,) * len(arrays),
        scratch_shapes=[pltpu.VMEM(array.shape, array.dtype) for array in arrays]
        + [pltpu.SemaphoreType.DMA((len(cuts),))] * 2,
    )(*arrays)


def shards(tokens, route_expert, hidden_grad, gate_weight, up_weight):
    vmem, anywhere = pl.BlockSpec(memory_space=pltpu.VMEM), pl.BlockSpec(memory_space=pl.ANY)
    tok_count = tokens.shape[0]
    dma = pltpu.SemaphoreType.DMA
    token_grad, gate_grad, up_grad = pl.pallas_call(
        kernel,
        out_shape=(
            jax.ShapeDtypeStruct(tokens.shape[::-1], BF),
            jax.ShapeDtypeStruct(gate_weight.shape, F32),
            jax.ShapeDtypeStruct(up_weight.shape, F32),
        ),
        in_specs=[anywhere] * 5,
        out_specs=(vmem, anywhere, anywhere),
        scratch_shapes=[
            pltpu.VMEM((1, tok_count), jnp.int32),
            pltpu.VMEM((ROW, tok_count), BF),
            pltpu.VMEM((GROUP, tok_count, LANE), BF),
            pltpu.VMEM(gate_weight.shape, BF),
            pltpu.VMEM(up_weight.shape, BF),
            pltpu.VMEM(gate_weight.shape, F32),
            pltpu.VMEM(up_weight.shape, F32),
            pltpu.VMEM((6, HALVES * BLOCK, NZ * IN_ROWS), BF),
            pltpu.VMEM((4, NZ * OUT_ROWS, HALVES * BLOCK), BF),
            pltpu.VMEM((NZ * OUT_ROWS, 4 * tok_count), BF),
            pltpu.VMEM((ROW, WIDE), BF),
            pltpu.VMEM((NZ, IN_ROWS, LANE), BF),
            pltpu.VMEM((NZ, IN_ROWS, LANE), BF),
            pltpu.VMEM((NY, BLOCK, ROW), BF),
            pltpu.VMEM((NY, BLOCK, ROW), BF),
            pltpu.VMEM((PAIRS, BLOCK, WIDE), F32),
            pltpu.VMEM((PAIRS, BLOCK, WIDE), F32),
            pltpu.VMEM((PAIRS, NX, BLOCK, LANE), F32),
            pltpu.VMEM((PAIRS, NX, BLOCK, LANE), BF),
            pltpu.VMEM((PAIRS, NX, BLOCK, LANE), BF),
            pltpu.VMEM((NY, NX, BLOCK, LANE), BF),
            pltpu.VMEM((NY, BLOCK, ROW), BF),
            pltpu.VMEM((NY, BLOCK, ROW), BF),
            pltpu.VMEM((NZ, OUT_ROWS, LANE), BF),
            pltpu.VMEM((NZ, OUT_ROWS, LANE), BF),
            dma((8,)),
            dma((NZ,)), dma((NZ,)),
            dma((NY,)), dma((NY,)),
            dma((PAIRS,)), dma((PAIRS,)),
            dma((PAIRS, NX)), dma((PAIRS, NX)),
            dma((PAIRS, NX)), dma((PAIRS, NX)),
            dma((PAIRS, NX)), dma((PAIRS, NX)),
            dma((NY,)), dma((NY,)),
            dma((NZ,)), dma((NZ,)),
        ],
        compiler_params=pltpu.CompilerParams(
            collective_id=0, has_side_effects=True, vmem_limit_bytes=56 * 1024 * 1024
        ),
    )(route_expert.reshape(1, -1), tokens.T, hidden_grad, gate_weight, up_weight)
    token_grad, gate_grad, up_grad = hand_over((token_grad, gate_grad, up_grad))
    return token_grad.T, gate_grad, up_grad


def solution(mesh):
    in_specs = (
        P("node", "local"),
        P("node"),
        P("node", None),
        P("local", "node"),
        P("local", "node"),
    )
    out_specs = (P("node", "local"), P("local", "node"), P("local", "node"))
    return jax.shard_map(shards, mesh=mesh, in_specs=in_specs, out_specs=out_specs, check_vma=False)
```
